32 devices in a mesh: gz: 4 (over z), gx: 2 (over y), gy: 4 (over x, core).
Axes of the slice: x: 2, y: 2, z: 4, core: 2. Of those that a mesh axis runs over, the one named last changes fastest.
Arguments:
- hydro_state: float32 [8, 32, 128, 512], P(None, 'gx', 'gy', 'gz'), may hold values from -0.5 to 2, as said below
- material_id: int32 [32, 128, 512], P('gx', 'gy', 'gz'), may hold values from 0 to 3
- block_mask: int32 [1, 4, 16], replicated, may hold values 0 or 1
Outputs:
- hydro_next: float32 [8, 32, 128, 512], P(None, 'gx', 'gy', 'gz')
The draws below stay inside these ranges and needn't reach their ends.
Inputs may be any that keep to these rules, and one draw needn't show every extreme that they name: `hydro_state`: field 0 lies in 0.9 to 2.0, fields 1 to 3 in -0.5 to 0.5, field 4 in 0.25 to 1.5, fields 5 and 7 in 0 to 1, field 6 in 0 to 0.5.
All inputs are finite; a program needn't handle non-finite values. Where the reference program divides by a largest or mean magnitude, that divisor is 1e-20 or more.
Results may differ from the reference program's by a relative error of at most 0.00011.
Values sent between devices are 32-bit elements; how exact they have to be, the bound alone decides.
A program may use at most 128 MiB of HBM per device.

```python
import jax
import jax.numpy as jnp

B = 32
CYCLES = 2
NMAT = 4
NX = 32
NY = 128
NZ = 512


def draw_hydro_state(key, part):
    subkeys = jax.random.split(key, 9)
    grid_shape = (NX, NY, NZ)
    centre = jax.random.uniform(subkeys[6], (), jnp.float32, 0.2, 0.8)
    speed_peak = jax.random.uniform(subkeys[7], (), jnp.float32, 0.6, 1.0)
    density_peak = jax.random.uniform(subkeys[8], (), jnp.float32, 0.5, 1.0)
    position = (jnp.arange(NZ, dtype=jnp.float32) + 0.5) / NZ
    profile = jnp.exp(-jnp.square((position - centre) / 0.12))
    speed_factor = (0.2 + 0.8 * speed_peak * profile)[None, None, None, :]
    density_span = (0.2 + 0.9 * density_peak * profile)[None, None, :]
    density = 0.9 + density_span * jax.random.uniform(subkeys[0], grid_shape, jnp.float32, 0.0, 1.0)
    velocity = jnp.clip(0.25 * jax.random.normal(subkeys[1], (3,) + grid_shape, jnp.float32), -0.5, 0.5) * speed_factor
    energy = jax.random.uniform(subkeys[2], grid_shape, jnp.float32, 0.5, 1.5)
    fraction = jax.random.uniform(subkeys[3], grid_shape, jnp.float32, 0.0, 1.0)
    plastic = jax.random.uniform(subkeys[4], grid_shape, jnp.float32, 0.0, 0.5)
    damage = jax.random.uniform(subkeys[5], grid_shape, jnp.float32, 0.0, 1.0)
    return jnp.concatenate([density[None], velocity, energy[None], fraction[None], plastic[None], damage[None]])


def touch_ends(entries, rng, least, high):
    spot = [jax.random.randint(jax.random.fold_in(rng, axis), (), 0, length) for axis, length in enumerate(entries.shape)]
    main_axis = entries.shape.index(max(entries.shape))
    beside = spot[:main_axis] + [(spot[main_axis] + 1) % entries.shape[main_axis]] + spot[main_axis + 1:]
    return entries.at[tuple(spot)].set(least).at[tuple(beside)].set(high)


def setup_inputs(seed: int = 0) -> dict:
    keys = jax.random.split(jax.random.key(seed), 4)
    return {
        "hydro_state": draw_hydro_state(jax.random.fold_in(keys[3], 71), 0),
        "material_id": touch_ends(jax.random.randint(keys[1], (NX, NY, NZ), 0, NMAT), jax.random.fold_in(keys[1], 1), 0, NMAT - 1).astype(jnp.int32),
        "block_mask": touch_ends((jax.random.randint(keys[2], (NX // B, NY // B, NZ // B), 0, 5) < 3).astype(jnp.int32), jax.random.fold_in(keys[2], 1), 0, 1),
    }


courant = 0.15
visc_quad = 2.0
visc_linear = 0.5
rest_density = (1.0, 1.25, 1.5, 1.8)
sound_base = (1.0, 0.8, 1.2, 0.9)
hugoniot_slope = (1.5, 1.4, 1.2, 1.6)
gruneisen = (2.0, 1.7, 1.6, 2.2)


def lookup(material, values):
    result = jnp.zeros(material.shape, jnp.float32)
    for number, amount in enumerate(values):
        result = result + jnp.where(material == number, jnp.float32(amount), jnp.float32(0.0))
    return result


def equation_of_state(density, energy, material):
    rest_rho = lookup(material, rest_density)
    sound_zero = lookup(material, sound_base)
    slope_mat = lookup(material, hugoniot_slope)
    gamma_mat = lookup(material, gruneisen)
    strain = 1.0 - rest_rho / density
    squeeze = jnp.maximum(strain, 0.0)
    hugoniot = rest_rho * sound_zero * sound_zero * strain * (1.0 + 2.0 * slope_mat * squeeze + 3.0 * slope_mat * slope_mat * squeeze * squeeze)
    pressure = hugoniot * (1.0 - 0.5 * gamma_mat * strain) + gamma_mat * density * energy
    sound_speed = sound_zero * (1.0 + slope_mat * squeeze)
    return pressure, sound_speed


def shifted(padded, spatial_axis, offset):
    starts = [1, 1, 1]
    starts[spatial_axis] = 1 + offset
    return padded[..., starts[0]:starts[0] + padded.shape[-3] - 2, starts[1]:starts[1] + padded.shape[-2] - 2, starts[2]:starts[2] + padded.shape[-1] - 2]


def stress_terms(velocity_pad, density, pressure, sound_speed):
    gradient = [(shifted(velocity_pad, column, 1) - shifted(velocity_pad, column, -1)) * 0.5 for column in range(3)]
    diverge = gradient[0][0] + gradient[1][1] + gradient[2][2]
    strain_xy = 0.5 * (gradient[1][0] + gradient[0][1])
    strain_xz = 0.5 * (gradient[2][0] + gradient[0][2])
    strain_yz = 0.5 * (gradient[2][1] + gradient[1][2])
    squares = gradient[0][0] * gradient[0][0] + gradient[1][1] * gradient[1][1] + gradient[2][2] * gradient[2][2]
    squares = squares + 2.0 * (strain_xy * strain_xy + strain_xz * strain_xz + strain_yz * strain_yz)
    compress = jnp.maximum(-diverge, 0.0)
    viscosity = density * compress * (visc_quad * compress + visc_linear * sound_speed)
    stress = jnp.stack([-pressure + viscosity * gradient[0][0], -pressure + viscosity * gradient[1][1], -pressure + viscosity * gradient[2][2], viscosity * strain_xy, viscosity * strain_xz, viscosity * strain_yz])
    power = -pressure * diverge + viscosity * squares
    heating = viscosity * squares
    return stress, diverge, power, heating


def acceleration(stress_pad, density):
    component_rows = ((0, 3, 4), (3, 1, 5), (4, 5, 2))
    results = []
    for comps in component_rows:
        total = jnp.zeros(density.shape, jnp.float32)
        for column in range(3):
            total = total + shifted(stress_pad[comps[column]], column, 1) - shifted(stress_pad[comps[column]], column, -1)
        results.append(0.5 * total / density)
    return jnp.stack(results)


def lagrange(state_part, density, accel, diverge, power, heating, step_dt):
    new_density = density / (1.0 + step_dt * diverge)
    velocity = state_part[1:4] + step_dt * accel
    energy = state_part[4] + step_dt * power / density
    plastic = state_part[6] + step_dt * heating / density
    return jnp.concatenate([new_density[None], new_density[None] * velocity, (new_density * energy)[None], (new_density * state_part[5])[None], (new_density * plastic)[None], (new_density * state_part[7])[None]])


def remap(conserved_pad, velocity_pad, step_dt):
    centre = shifted(conserved_pad, 0, 0)
    total = centre
    for column in range(3):
        middle_vel = shifted(velocity_pad[column], column, 0)
        ahead_vel = shifted(velocity_pad[column], column, 1)
        behind_vel = shifted(velocity_pad[column], column, -1)
        upper = step_dt * 0.5 * (middle_vel + ahead_vel)
        lower = step_dt * 0.5 * (behind_vel + middle_vel)
        flux_up = jnp.maximum(upper, 0.0) * centre + jnp.minimum(upper, 0.0) * shifted(conserved_pad, column, 1)
        flux_down = jnp.maximum(lower, 0.0) * shifted(conserved_pad, column, -1) + jnp.minimum(lower, 0.0) * centre
        total = total - (flux_up - flux_down)
    density = total[0]
    return jnp.concatenate([density[None], total[1:] / density])


def cell_mask(block_mask, edge):
    count_x, count_y, count_z = block_mask.shape
    spread = jnp.broadcast_to(block_mask[:, None, :, None, :, None], (count_x, edge, count_y, edge, count_z, edge))
    return spread.reshape(count_x * edge, count_y * edge, count_z * edge) > 0


def pad_one(array_in):
    return jnp.pad(array_in, ((0, 0), (1, 1), (1, 1), (1, 1)))


def reference(hydro_state, material_id, block_mask):
    active = cell_mask(block_mask, B)
    state_now = hydro_state
    for cycle_number in range(CYCLES):
        pressure, sound_speed = equation_of_state(state_now[0], state_now[4], material_id)
        fastest = jnp.max(sound_speed + jnp.abs(state_now[1]) + jnp.abs(state_now[2]) + jnp.abs(state_now[3]))
        step_dt = courant / fastest
        velocity_pad = pad_one(state_now[1:4])
        stress, diverge, power, heating = stress_terms(velocity_pad, state_now[0], pressure, sound_speed)
        accel = acceleration(pad_one(stress), state_now[0])
        conserved = lagrange(state_now, state_now[0], accel, diverge, power, heating, step_dt)
        remapped = remap(pad_one(conserved), velocity_pad, step_dt)
        state_now = jnp.where(active[None], remapped, state_now)
    return state_now
```

```python
import functools

import jax
import jax.numpy as jnp
from jax import lax
from jax.experimental import pallas as pl
from jax.experimental.pallas import tpu as pltpu
from jax.sharding import PartitionSpec as P

B = 32
CYCLES = 2
AXES = ("gx", "gy", "gz")
HALVES = 2
PAD = 8
TILE = 32
MESH = pl.DeviceIdType.MESH

courant = 0.15
visc_quad = 2.0
visc_linear = 0.5
rest_density = (1.0, 1.25, 1.5, 1.8)
sound_base = (1.0, 0.8, 1.2, 0.9)
hugoniot_slope = (1.5, 1.4, 1.2, 1.6)
gruneisen = (2.0, 1.7, 1.6, 2.2)
stiffness = tuple(r * c * c for r, c in zip(rest_density, sound_base))

STRESS = ((0, 1, 2), (1, 3, 4), (2, 4, 5))
COUNT = (3, 3, 8)


def pick(is_one, is_two, is_three, table):
    return jnp.where(
        is_three, table[3], jnp.where(is_two, table[2], jnp.where(is_one, table[1], table[0]))
    )


def equation_of_state(density, inverse, energy, material):
    tests = (material == 1, material == 2, material == 3)
    rest_rho = pick(*tests, rest_density)
    sound_zero = pick(*tests, sound_base)
    slope = pick(*tests, hugoniot_slope)
    gamma = pick(*tests, gruneisen)
    stiff = pick(*tests, stiffness)
    strain = 1.0 - rest_rho * inverse
    climb = slope * jnp.maximum(strain, 0.0)
    hugoniot = stiff * strain * (1.0 + climb * (2.0 + 3.0 * climb))
    pressure = hugoniot * (1.0 - 0.5 * gamma * strain) + gamma * density * energy
    return pressure, sound_zero + sound_zero * climb


def kernel(
    sizes, mask_ref, state_hbm, material_hbm, out_ref,
    vel, stress, cons, scal, inv, mat, pres, sound, terms,
    ys0, ys1, ys2, yr0, yr1, yr2, zs, zr, zc, peak, step,
    load_sem, send_sem, recv_sem, peak_send, peak_recv,
):
    _, nx, ny, nz = state_hbm.shape
    half = nx // HALVES
    index = {axis: lax.axis_index(axis) for axis in AXES}
    above = {axis: index[axis] < sizes[axis] - 1 for axis in AXES}
    below = {axis: index[axis] > 0 for axis in AXES}
    ys, yr = (ys0, ys1, ys2), (yr0, yr1, yr2)
    buffers = (vel, stress, cons)
    inner = pl.ds(PAD, ny)

    loads = [
        pltpu.make_async_copy(state_hbm.at[1:4], vel.at[0, :, 1 : nx + 1, PAD : PAD + ny], load_sem.at[0]),
        pltpu.make_async_copy(state_hbm.at[0:1], scal.at[0:1], load_sem.at[1]),
        pltpu.make_async_copy(state_hbm.at[4:8], scal.at[1:5], load_sem.at[2]),
        pltpu.make_async_copy(material_hbm, mat, load_sem.at[3]),
    ]
    for load in loads:
        load.start()

    barrier = pltpu.get_barrier_semaphore()
    total = 0
    for axis in AXES:
        for away in range(1, sizes[axis]):
            peer = lax.rem(index[axis] + away, sizes[axis])
            pl.semaphore_signal(barrier, inc=1, device_id={axis: peer}, device_id_type=MESH)
            total += 1

    for axis_number, axis in enumerate(AXES):
        for side, exists in ((0, below[axis]), (1, above[axis])):

            @pl.when(jnp.logical_not(exists))
            def _(axis_number=axis_number, side=side):
                for cycle in range(CYCLES):
                    for r in range(3):
                        if axis_number == 0:
                            ghost = (nx + 1) * side
                            for f in range(COUNT[r]):
                                buffers[r][cycle, f, ghost, inner, :] = jnp.zeros((ny, nz), jnp.float32)
                        elif axis_number == 1:
                            yr[r][cycle, side] = jnp.zeros(yr[r].shape[2:], jnp.float32)
                        else:
                            zr[cycle, r, :, side] = jnp.zeros((HALVES, ny, nz), jnp.float32)

    zs[...] = jnp.zeros_like(zs)
    for cycle in range(CYCLES):
        peak[cycle, 0, 0] = jnp.zeros((8, nz), jnp.float32)

    def copy(cycle, r, slot, side, src, dst, axis):
        move = 1 if side == 0 else sizes[axis] - 1
        return pltpu.make_async_remote_copy(
            src_ref=src,
            dst_ref=dst,
            send_sem=send_sem.at[cycle, r, slot],
            recv_sem=recv_sem.at[cycle, r, slot],
            device_id={axis: lax.rem(index[axis] + move, sizes[axis])},
            device_id_type=MESH,
        )

    def x_copy(cycle, r, side):
        own, ghost = (nx, 0) if side == 0 else (1, nx + 1)
        part = buffers[r].at[cycle, 0 : COUNT[r]]
        return copy(
            cycle, r, side, side,
            part.at[:, own, PAD : PAD + ny], part.at[:, ghost, PAD : PAD + ny], "gx",
        )

    def y_copy(cycle, r, h, side):
        rows = slice(h * half, (h + 1) * half)
        return copy(
            cycle, r, 2 + 4 * h + side, side,
            ys[r].at[cycle, side, :, rows], yr[r].at[cycle, side, :, rows], "gy",
        )

    def z_copy(cycle, r, h, side):
        return copy(
            cycle, r, 4 + 4 * h + side, side, zs.at[cycle, r, h], zr.at[cycle, r, h, side], "gz"
        )

    def for_side(exists, axis, act):
        if sizes[axis] > 1:
            pl.when(exists)(act)

    def send(cycle, r, h):
        side = 1 - h
        for_side((above if side == 0 else below)["gx"], "gx", lambda: x_copy(cycle, r, side).start())
        for s in range(2):
            way = above if s == 0 else below
            for_side(way["gy"], "gy", lambda: y_copy(cycle, r, h, s).start())
            for_side(way["gz"], "gz", lambda: z_copy(cycle, r, h, s).start())

    lane = lax.broadcasted_iota(jnp.int32, (TILE, nz), 1)
    first_lane, last_lane = lane == 0, lane == nz - 1
    pair = lane // 2

    def receive(cycle, r, h):
        for_side((below if h == 0 else above)["gx"], "gx", lambda: x_copy(cycle, r, h).wait_recv())
        for s in range(2):
            way = below if s == 0 else above
            for_side(way["gy"], "gy", lambda: y_copy(cycle, r, h, s).wait_recv())
            for_side(way["gz"], "gz", lambda: z_copy(cycle, r, h, s).wait_recv())
        fields = STRESS[1] if r == 1 else range(COUNT[r])

        def spread(i, carry):
            x = h * half + i
            for n, f in enumerate(fields):
                buffers[r][cycle, f, x + 1, pl.ds(PAD - 1, 1), :] = yr[r][cycle, 0, n, pl.ds(x, 1), :]
                buffers[r][cycle, f, x + 1, pl.ds(PAD + ny, 1), :] = yr[r][cycle, 1, n, pl.ds(x, 1), :]
            return carry

        lax.fori_loop(0, half, spread, 0)
        odd = lax.broadcasted_iota(jnp.int32, (ny, nz), 1) % 2 == 1
        zc[cycle, r, h] = jnp.where(
            odd, pltpu.roll(zr[cycle, r, h, 0], 1, 1), pltpu.roll(zr[cycle, r, h, 1], nz - 1, 1)
        )

    def pack(cycle, r, h, x, y0, values):
        rows = pl.ds(y0, TILE)
        edge = zs[cycle, r, h, rows, :]
        for n, value in enumerate(values):
            slot = (x - h * half) * len(values) + n
            edge = jnp.where(pair == slot, pltpu.roll(value, 2 * slot + 1, 1), edge)
        zs[cycle, r, h, rows, :] = edge

    def pack_rows(cycle, r, x, y0, values):
        for n, value in enumerate(values):
            if y0 + TILE == ny:
                ys[r][cycle, 0, n, pl.ds(x, 1), :] = value[TILE - 1 : TILE]
            if y0 == 0:
                ys[r][cycle, 1, n, pl.ds(x, 1), :] = value[0:1]

    def at(r, cycle, f, x, y0, dx=0, dy=0):
        return buffers[r][cycle, f, x + 1 + dx, pl.ds(PAD + y0 + dy, TILE), :]

    def z_pair(cycle, r, h, x, y0, n, value):
        slot = (x - h * half) * COUNT[r] + n
        ghost = pltpu.roll(zc[cycle, r, h, pl.ds(y0, TILE), :], nz - 1 - 2 * slot, 1)
        ahead = jnp.where(last_lane, ghost, pltpu.roll(value, nz - 1, 1))
        behind = jnp.where(first_lane, ghost, pltpu.roll(value, 1, 1))
        return ahead, behind

    def planes(h, body):
        def run(i, carry):
            x = h * half + i
            for y0 in range(0, ny, TILE):
                body(h, x, y0)
            return carry

        lax.fori_loop(0, half, run, 0)

    def begin(cycle, h, x, y0, density, inverse, energy, velocity):
        rows = pl.ds(y0, TILE)
        pressure, speed = equation_of_state(density, inverse, energy, mat[x, rows, :])
        pres[x, rows, :] = pressure
        sound[x, rows, :] = speed
        fast = speed + jnp.abs(velocity[0]) + jnp.abs(velocity[1]) + jnp.abs(velocity[2])
        top = peak[cycle, 0, 0]
        for r0 in range(0, TILE, 8):
            top = jnp.maximum(top, fast[r0 : r0 + 8])
        peak[cycle, 0, 0] = top
        pack(cycle, 0, h, x, y0, velocity)
        pack_rows(cycle, 0, x, y0, velocity)

    def stage_start(h, x, y0):
        rows = pl.ds(y0, TILE)
        density = scal[0, x, rows, :]
        inverse = 1.0 / density
        inv[x, rows, :] = inverse
        begin(0, h, x, y0, density, inverse, scal[1, x, rows, :], [at(0, 0, f, x, y0) for f in range(3)])

    def stage_stress(cycle, h, x, y0):
        rows = pl.ds(y0, TILE)
        g = []
        for f in range(3):
            ahead, behind = z_pair(cycle, 0, h, x, y0, f, at(0, cycle, f, x, y0))
            g.append((
                at(0, cycle, f, x, y0, dx=1) - at(0, cycle, f, x, y0, dx=-1),
                at(0, cycle, f, x, y0, dy=1) - at(0, cycle, f, x, y0, dy=-1),
                ahead - behind,
            ))
        div = 0.5 * (g[0][0] + g[1][1] + g[2][2])
        sxy, sxz, syz = g[0][1] + g[1][0], g[0][2] + g[2][0], g[1][2] + g[2][1]
        squares = 0.25 * (
            g[0][0] * g[0][0] + g[1][1] * g[1][1] + g[2][2] * g[2][2]
            + 0.5 * (sxy * sxy + sxz * sxz + syz * syz)
        )
        pressure = pres[x, rows, :]
        squash = jnp.maximum(-div, 0.0)
        mu = scal[0, x, rows, :] * squash * (visc_quad * squash + visc_linear * sound[x, rows, :])
        whole, quarter = 0.5 * mu, 0.25 * mu
        values = (
            whole * g[0][0] - pressure, quarter * sxy, quarter * sxz,
            whole * g[1][1] - pressure, quarter * syz, whole * g[2][2] - pressure,
        )
        for f, value in enumerate(values):
            stress[cycle, f, x + 1, pl.ds(PAD + y0, TILE), :] = value
        heat = mu * squares
        terms[0, x, rows, :] = div
        terms[1, x, rows, :] = heat - pressure * div
        terms[2, x, rows, :] = heat
        pack(cycle, 1, h, x, y0, [values[f] for f in STRESS[2]])
        pack_rows(cycle, 1, x, y0, [values[f] for f in STRESS[1]])

    def stage_conserved(cycle, h, x, y0):
        rows = pl.ds(y0, TILE)
        dt = step[0:1, :]
        inverse = inv[x, rows, :]
        scaled = dt * inverse
        density = scal[0, x, rows, :] / (1.0 + dt * terms[0, x, rows, :])
        values = [density]
        for i in range(3):
            fx, fy, fz = STRESS[i]
            ahead, behind = z_pair(cycle, 1, h, x, y0, i, at(1, cycle, fz, x, y0))
            force = (
                (at(1, cycle, fx, x, y0, dx=1) - at(1, cycle, fx, x, y0, dx=-1))
                + (at(1, cycle, fy, x, y0, dy=1) - at(1, cycle, fy, x, y0, dy=-1))
                + (ahead - behind)
            )
            values.append(density * (at(0, cycle, i, x, y0) + (0.5 * scaled) * force))
        values.append(density * (scal[1, x, rows, :] + scaled * terms[1, x, rows, :]))
        values.append(density * scal[2, x, rows, :])
        values.append(density * (scal[3, x, rows, :] + scaled * terms[2, x, rows, :]))
        values.append(density * scal[4, x, rows, :])
        for f, value in enumerate(values):
            cons[cycle, f, x + 1, pl.ds(PAD + y0, TILE), :] = value
        pack(cycle, 2, h, x, y0, values)
        pack_rows(cycle, 2, x, y0, values)

    present = jnp.zeros((1, nz), jnp.int32)
    block = lax.broadcasted_iota(jnp.int32, (1, nz), 1) // B
    for j in range(nz // B):
        value = mask_ref[index["gx"] * nx // B, index["gy"] * ny // B, index["gz"] * (nz // B) + j]
        present = jnp.where(block == j, value, present)

    def stage_remap(cycle, h, x, y0):
        rows = pl.ds(y0, TILE)
        active = jnp.broadcast_to(present, (TILE, nz)) > 0
        half_dt = 0.5 * step[0:1, :]
        velocity = [at(0, cycle, f, x, y0) for f in range(3)]
        z_ahead, z_behind = z_pair(cycle, 0, h, x, y0, 2, velocity[2])
        around = (
            (at(0, cycle, 0, x, y0, dx=1), at(0, cycle, 0, x, y0, dx=-1)),
            (at(0, cycle, 1, x, y0, dy=1), at(0, cycle, 1, x, y0, dy=-1)),
            (z_ahead, z_behind),
        )
        centre = 1.0
        into = []
        for j in range(3):
            upper = half_dt * (velocity[j] + around[j][0])
            lower = half_dt * (around[j][1] + velocity[j])
            up_in, down_in = jnp.minimum(upper, 0.0), jnp.maximum(lower, 0.0)
            centre = centre - (jnp.maximum(upper, 0.0) - jnp.minimum(lower, 0.0))
            into.append((up_in, down_in))

        def result(f):
            value = at(2, cycle, f, x, y0)
            ahead, behind = z_pair(cycle, 2, h, x, y0, f, value)
            return (
                centre * value
                - (into[0][0] * at(2, cycle, f, x, y0, dx=1) - into[0][1] * at(2, cycle, f, x, y0, dx=-1))
                - (into[1][0] * at(2, cycle, f, x, y0, dy=1) - into[1][1] * at(2, cycle, f, x, y0, dy=-1))
                - (into[2][0] * ahead - into[2][1] * behind)
            )

        density = result(0)
        inverse = 1.0 / density
        old = [scal[0, x, rows, :]] + velocity + [scal[n, x, rows, :] for n in range(1, 5)]
        new = [jnp.where(active, density, old[0])]
        for f in range(1, 8):
            new.append(jnp.where(active, result(f) * inverse, old[f]))
        if cycle == CYCLES - 1:
            for f in range(8):
                out_ref[f, x, rows, :] = new[f]
            return
        for n, f in enumerate((0, 4, 5, 6, 7)):
            scal[n, x, rows, :] = new[f]
        for f in range(3):
            vel[cycle + 1, f, x + 1, pl.ds(PAD + y0, TILE), :] = new[f + 1]
        inverse = jnp.where(active, inverse, inv[x, rows, :])
        inv[x, rows, :] = inverse
        begin(cycle + 1, h, x, y0, new[0], inverse, new[4], new[1:4])

    def peak_copy(cycle, phase, away):
        axis = AXES[2 - phase]
        return pltpu.make_async_remote_copy(
            src_ref=peak.at[cycle, phase, 0],
            dst_ref=peak.at[cycle, phase, away],
            send_sem=peak_send.at[cycle, phase, away],
            recv_sem=peak_recv.at[cycle, phase, away],
            device_id={axis: lax.rem(index[axis] + away, sizes[axis])},
            device_id_type=MESH,
        )

    def peak_send_all(cycle, phase):
        for away in range(1, sizes[AXES[2 - phase]]):
            peak_copy(cycle, phase, away).start()

    def peak_take(cycle, phase):
        top = peak[cycle, phase, 0]
        for away in range(1, sizes[AXES[2 - phase]]):
            peak_copy(cycle, phase, away).wait_recv()
            top = jnp.maximum(top, peak[cycle, phase, away])
        if phase < 2:
            peak[cycle, phase + 1, 0] = top
        else:
            fastest = jnp.max(jnp.max(top, axis=1, keepdims=True), axis=0, keepdims=True)
            step[...] = courant / jnp.broadcast_to(fastest, step.shape)

    for load in loads:
        load.wait()
    pl.semaphore_wait(barrier, total)

    for h in range(HALVES):
        planes(h, stage_start)
        send(0, 0, h)
    for cycle in range(CYCLES):
        peak_send_all(cycle, 0)
        for h in range(HALVES):
            receive(cycle, 0, h)
            planes(h, functools.partial(stage_stress, cycle))
            send(cycle, 1, h)
            peak_take(cycle, h)
            peak_send_all(cycle, h + 1)
        peak_take(cycle, 2)
        for h in range(HALVES):
            receive(cycle, 1, h)
            planes(h, functools.partial(stage_conserved, cycle))
            send(cycle, 2, h)
        for h in range(HALVES):
            receive(cycle, 2, h)
            planes(h, functools.partial(stage_remap, cycle))
            if cycle + 1 < CYCLES:
                send(cycle + 1, 0, h)

    for cycle in range(CYCLES):
        for phase in range(3):
            for away in range(1, sizes[AXES[2 - phase]]):
                peak_copy(cycle, phase, away).wait_send()
        for r in range(3):
            for s in range(2):
                way = above if s == 0 else below
                for_side(way["gx"], "gx", lambda: x_copy(cycle, r, s).wait_send())
                for h in range(HALVES):
                    for_side(way["gy"], "gy", lambda: y_copy(cycle, r, h, s).wait_send())
                    for_side(way["gz"], "gz", lambda: z_copy(cycle, r, h, s).wait_send())


def solution(mesh):
    sizes = {axis: mesh.shape[axis] for axis in AXES}

    def local(hydro_state, material_id, block_mask):
        _, nx, ny, nz = hydro_state.shape
        f32 = jnp.float32
        most = max(sizes.values())
        padded = (nx + 2, ny + 2 * PAD, nz)
        body = (nx, ny, nz)
        scratch = [
            pltpu.VMEM((CYCLES, 3) + padded, f32),
            pltpu.VMEM((CYCLES, 6) + padded, f32),
            pltpu.VMEM((CYCLES, 8) + padded, f32),
            pltpu.VMEM((5,) + body, f32),
            pltpu.VMEM(body, f32),
            pltpu.VMEM(body, jnp.int32),
            pltpu.VMEM(body, f32),
            pltpu.VMEM(body, f32),
            pltpu.VMEM((3,) + body, f32),
        ]
        for _ in range(2):
            scratch += [pltpu.VMEM((CYCLES, 2, count, nx, nz), f32) for count in COUNT]
        scratch += [
            pltpu.VMEM((CYCLES, 3, HALVES, ny, nz), f32),
            pltpu.VMEM((CYCLES, 3, HALVES, 2, ny, nz), f32),
            pltpu.VMEM((CYCLES, 3, HALVES, ny, nz), f32),
            pltpu.VMEM((CYCLES, 3, most, 8, nz), f32),
            pltpu.VMEM((8, nz), f32),
            pltpu.SemaphoreType.DMA((4,)),
            pltpu.SemaphoreType.DMA((CYCLES, 3, 2 + 4 * HALVES)),
            pltpu.SemaphoreType.DMA((CYCLES, 3, 2 + 4 * HALVES)),
            pltpu.SemaphoreType.DMA((CYCLES, 3, most)),
            pltpu.SemaphoreType.DMA((CYCLES, 3, most)),
        ]
        return pl.pallas_call(
            functools.partial(kernel, sizes),
            out_shape=jax.ShapeDtypeStruct(hydro_state.shape, f32),
            in_specs=[
                pl.BlockSpec(memory_space=pltpu.SMEM),
                pl.BlockSpec(memory_space=pl.ANY),
                pl.BlockSpec(memory_space=pl.ANY),
            ],
            out_specs=pl.BlockSpec(memory_space=pltpu.VMEM),
            scratch_shapes=scratch,
            compiler_params=pltpu.CompilerParams(
                collective_id=0, has_side_effects=True, vmem_limit_bytes=48 * 1024 * 1024
            ),
        )(block_mask, hydro_state, material_id)

    in_specs = (P(None, "gx", "gy", "gz"), P("gx", "gy", "gz"), P())
    out_specs = P(None, "gx", "gy", "gz")
    return jax.shard_map(local, mesh=mesh, in_specs=in_specs, out_specs=out_specs, check_vma=False)
```

```python
import functools

import jax
import jax.numpy as jnp
from jax import lax
from jax.experimental import pallas as pl
from jax.experimental.pallas import tpu as pltpu
from jax.sharding import PartitionSpec as P

B = 32
CYCLES = 2
AXES = ("gx", "gy", "gz")
HALVES = 2
PAD = 8
TILE = 32
GROUP = 2
MESH = pl.DeviceIdType.MESH

courant = 0.15
visc_quad = 2.0
visc_linear = 0.5
rest_density = (1.0, 1.25, 1.5, 1.8)
sound_base = (1.0, 0.8, 1.2, 0.9)
hugoniot_slope = (1.5, 1.4, 1.2, 1.6)
gruneisen = (2.0, 1.7, 1.6, 2.2)
stiffness = tuple(r * c * c for r, c in zip(rest_density, sound_base))

STRESS = ((0, 1, 2), (1, 3, 4), (2, 4, 5))
COUNT = (3, 3, 8)


def pick(is_one, is_two, is_three, table):
    return jnp.where(
        is_three, table[3], jnp.where(is_two, table[2], jnp.where(is_one, table[1], table[0]))
    )


def equation_of_state(density, inverse, energy, material):
    tests = (material == 1, material == 2, material == 3)
    rest_rho = pick(*tests, rest_density)
    sound_zero = pick(*tests, sound_base)
    slope = pick(*tests, hugoniot_slope)
    gamma = pick(*tests, gruneisen)
    stiff = pick(*tests, stiffness)
    strain = 1.0 - rest_rho * inverse
    climb = slope * jnp.maximum(strain, 0.0)
    hugoniot = stiff * strain * (1.0 + climb * (2.0 + 3.0 * climb))
    pressure = hugoniot * (1.0 - 0.5 * gamma * strain) + gamma * density * energy
    return pressure, sound_zero + sound_zero * climb


def kernel(
    sizes, mask_ref, state_hbm, material_hbm, out_ref,
    vel, stress, cons, scal, inv, mat, pres, sound, terms,
    ys0, ys1, ys2, yr0, yr1, yr2, zs, zr, zc, peak, step,
    load_sem, send_sem, recv_sem, peak_send, peak_recv,
):
    _, nx, ny, nz = state_hbm.shape
    half = nx // HALVES
    index = {axis: lax.axis_index(axis) for axis in AXES}
    above = {axis: index[axis] < sizes[axis] - 1 for axis in AXES}
    below = {axis: index[axis] > 0 for axis in AXES}
    ys, yr = (ys0, ys1, ys2), (yr0, yr1, yr2)
    buffers = (vel, stress, cons)
    inner = pl.ds(PAD, ny)

    loads = [
        pltpu.make_async_copy(state_hbm.at[1:4], vel.at[0, :, 1 : nx + 1, PAD : PAD + ny], load_sem.at[0]),
        pltpu.make_async_copy(state_hbm.at[0:1], scal.at[0:1], load_sem.at[1]),
        pltpu.make_async_copy(state_hbm.at[4:8], scal.at[1:5], load_sem.at[2]),
        pltpu.make_async_copy(material_hbm, mat, load_sem.at[3]),
    ]
    for load in loads:
        load.start()

    barrier = pltpu.get_barrier_semaphore()
    total = 0
    for axis in AXES:
        for away in range(1, sizes[axis]):
            peer = lax.rem(index[axis] + away, sizes[axis])
            pl.semaphore_signal(barrier, inc=1, device_id={axis: peer}, device_id_type=MESH)
            total += 1

    for axis_number, axis in enumerate(AXES):
        for side, exists in ((0, below[axis]), (1, above[axis])):

            @pl.when(jnp.logical_not(exists))
            def _(axis_number=axis_number, side=side):
                for cycle in range(CYCLES):
                    for r in range(3):
                        if axis_number == 0:
                            ghost = (nx + 1) * side
                            for f in range(COUNT[r]):
                                buffers[r][cycle, f, ghost, inner, :] = jnp.zeros((ny, nz), jnp.float32)
                        elif axis_number == 1:
                            yr[r][cycle, side] = jnp.zeros(yr[r].shape[2:], jnp.float32)
                        else:
                            zr[cycle, r, :, side] = jnp.zeros((HALVES, ny, nz), jnp.float32)

    def copy(cycle, r, slot, side, src, dst, axis):
        move = 1 if side == 0 else sizes[axis] - 1
        return pltpu.make_async_remote_copy(
            src_ref=src,
            dst_ref=dst,
            send_sem=send_sem.at[cycle, r, slot],
            recv_sem=recv_sem.at[cycle, r, slot],
            device_id={axis: lax.rem(index[axis] + move, sizes[axis])},
            device_id_type=MESH,
        )

    def x_copy(cycle, r, side):
        own, ghost = (nx, 0) if side == 0 else (1, nx + 1)
        part = buffers[r].at[cycle, 0 : COUNT[r]]
        return copy(
            cycle, r, side, side,
            part.at[:, own, PAD : PAD + ny], part.at[:, ghost, PAD : PAD + ny], "gx",
        )

    def y_copy(cycle, r, h, side):
        rows = slice(h * half, (h + 1) * half)
        return copy(
            cycle, r, 2 + 4 * h + side, side,
            ys[r].at[cycle, side, :, rows], yr[r].at[cycle, side, :, rows], "gy",
        )

    def z_copy(cycle, r, h, side):
        return copy(
            cycle, r, 4 + 4 * h + side, side, zs.at[cycle, r, h], zr.at[cycle, r, h, side], "gz"
        )

    def for_side(exists, axis, act):
        if sizes[axis] > 1:
            pl.when(exists)(act)

    def send_x(cycle, r, side):
        for_side((above if side == 0 else below)["gx"], "gx", lambda: x_copy(cycle, r, side).start())

    def receive_x(cycle, r, side):
        for_side((below if side == 0 else above)["gx"], "gx", lambda: x_copy(cycle, r, side).wait_recv())

    def send(cycle, r, h):
        if h == 0:
            send_x(cycle, r, 1)
        for s in range(2):
            way = above if s == 0 else below
            for_side(way["gy"], "gy", lambda: y_copy(cycle, r, h, s).start())
            for_side(way["gz"], "gz", lambda: z_copy(cycle, r, h, s).start())

    lane = lax.broadcasted_iota(jnp.int32, (TILE, nz), 1)
    first_lane, last_lane = lane == 0, lane == nz - 1
    pair = lane // 2

    def receive(cycle, r, h):
        if h == 1:
            receive_x(cycle, r, 1)
        for s in range(2):
            way = below if s == 0 else above
            for_side(way["gy"], "gy", lambda: y_copy(cycle, r, h, s).wait_recv())
            for_side(way["gz"], "gz", lambda: z_copy(cycle, r, h, s).wait_recv())
        fields = STRESS[1] if r == 1 else range(COUNT[r])

        for x in range(h * half, h * half + half):
            for n, f in enumerate(fields):
                buffers[r][cycle, f, x + 1, pl.ds(PAD - 1, 1), :] = yr[r][cycle, 0, n, pl.ds(x, 1), :]
                buffers[r][cycle, f, x + 1, pl.ds(PAD + ny, 1), :] = yr[r][cycle, 1, n, pl.ds(x, 1), :]

        odd = lax.broadcasted_iota(jnp.int32, (ny, nz), 1) % 2 == 1
        zc[cycle, r, h] = jnp.where(
            odd, pltpu.roll(zr[cycle, r, h, 0], 1, 1), pltpu.roll(zr[cycle, r, h, 1], nz - 1, 1)
        )

    def pack(h, x, edge, values):
        for n, value in enumerate(values):
            slot = (x - h * half) * len(values) + n
            edge = jnp.where(pair == slot, pltpu.roll(value, 2 * slot + 1, 1), edge)
        return edge

    def pack_rows(cycle, r, x, y0, values):
        for n, value in enumerate(values):
            if y0 + TILE == ny:
                ys[r][cycle, 0, n, pl.ds(x, 1), :] = value[TILE - 1 : TILE]
            if y0 == 0:
                ys[r][cycle, 1, n, pl.ds(x, 1), :] = value[0:1]

    def at(r, cycle, f, x, y0, dx=0, dy=0):
        return buffers[r][cycle, f, x + 1 + dx, pl.ds(PAD + y0 + dy, TILE), :]

    def z_pair(cycle, r, h, x, y0, n, value):
        slot = (x - h * half) * COUNT[r] + n
        ghost = pltpu.roll(zc[cycle, r, h, pl.ds(y0, TILE), :], nz - 1 - 2 * slot, 1)
        ahead = jnp.where(last_lane, ghost, pltpu.roll(value, nz - 1, 1))
        behind = jnp.where(first_lane, ghost, pltpu.roll(value, 1, 1))
        return ahead, behind

    def planes(h, body, cycle, gives, takes=None):
        groups = half // GROUP

        def run(i, carry):
            edge, top = carry
            if h == 0 and takes is not None:
                pl.when(i == groups - 1)(lambda: receive_x(cycle, takes, 0))
            for j in range(GROUP):
                edge, top = body(h, (h + 1) * half - 1 - (i * GROUP + j), edge, top)
            if h == 1 and gives is not None:
                pl.when(i == 0)(lambda: send_x(gives[0], gives[1], 0))
            return edge, top

        init = (jnp.zeros((ny, nz), jnp.float32), jnp.zeros((8, nz), jnp.float32))
        edge, top = lax.fori_loop(0, groups, run, init)
        if gives is not None:
            zs[gives[0], gives[1], h] = edge
            if gives[1] == 0:
                peak[gives[0], 0, 0] = top if h == 0 else jnp.maximum(peak[gives[0], 0, 0], top)
            send(gives[0], gives[1], h)

    def begin(cycle, h, x, edge, top, density, inverse, energy, velocity):
        y0 = 0
        rows = pl.ds(y0, TILE)
        pressure, speed = equation_of_state(density, inverse, energy, mat[x, rows, :])
        pres[x, rows, :] = pressure
        sound[x, rows, :] = speed
        fast = speed + jnp.abs(velocity[0]) + jnp.abs(velocity[1]) + jnp.abs(velocity[2])
        for r0 in range(0, TILE, 8):
            top = jnp.maximum(top, fast[r0 : r0 + 8])
        pack_rows(cycle, 0, x, y0, velocity)
        return pack(h, x, edge, velocity), top

    def stage_start(h, x, edge, top):
        y0 = 0
        rows = pl.ds(y0, TILE)
        density = scal[0, x, rows, :]
        inverse = 1.0 / density
        inv[x, rows, :] = inverse
        return begin(0, h, x, edge, top, density, inverse, scal[1, x, rows, :], [at(0, 0, f, x, y0) for f in range(3)])

    def stage_stress(cycle, h, x, edge, top):
        y0 = 0
        rows = pl.ds(y0, TILE)
        g = []
        for f in range(3):
            ahead, behind = z_pair(cycle, 0, h, x, y0, f, at(0, cycle, f, x, y0))
            g.append((
                at(0, cycle, f, x, y0, dx=1) - at(0, cycle, f, x, y0, dx=-1),
                at(0, cycle, f, x, y0, dy=1) - at(0, cycle, f, x, y0, dy=-1),
                ahead - behind,
            ))
        div = 0.5 * (g[0][0] + g[1][1] + g[2][2])
        sxy, sxz, syz = g[0][1] + g[1][0], g[0][2] + g[2][0], g[1][2] + g[2][1]
        squares = 0.25 * (
            g[0][0] * g[0][0] + g[1][1] * g[1][1] + g[2][2] * g[2][2]
            + 0.5 * (sxy * sxy + sxz * sxz + syz * syz)
        )
        pressure = pres[x, rows, :]
        squash = jnp.maximum(-div, 0.0)
        mu = scal[0, x, rows, :] * squash * (visc_quad * squash + visc_linear * sound[x, rows, :])
        whole, quarter = 0.5 * mu, 0.25 * mu
        values = (
            whole * g[0][0] - pressure, quarter * sxy, quarter * sxz,
            whole * g[1][1] - pressure, quarter * syz, whole * g[2][2] - pressure,
        )
        for f, value in enumerate(values):
            stress[cycle, f, x + 1, pl.ds(PAD + y0, TILE), :] = value
        heat = mu * squares
        terms[0, x, rows, :] = div
        terms[1, x, rows, :] = heat - pressure * div
        terms[2, x, rows, :] = heat
        pack_rows(cycle, 1, x, y0, [values[f] for f in STRESS[1]])
        return pack(h, x, edge, [values[f] for f in STRESS[2]]), top

    def stage_conserved(cycle, h, x, edge, top):
        y0 = 0
        rows = pl.ds(y0, TILE)
        dt = step[0:1, :]
        inverse = inv[x, rows, :]
        scaled = dt * inverse
        density = scal[0, x, rows, :] / (1.0 + dt * terms[0, x, rows, :])
        values = [density]
        for i in range(3):
            fx, fy, fz = STRESS[i]
            ahead, behind = z_pair(cycle, 1, h, x, y0, i, at(1, cycle, fz, x, y0))
            force = (
                (at(1, cycle, fx, x, y0, dx=1) - at(1, cycle, fx, x, y0, dx=-1))
                + (at(1, cycle, fy, x, y0, dy=1) - at(1, cycle, fy, x, y0, dy=-1))
                + (ahead - behind)
            )
            values.append(density * (at(0, cycle, i, x, y0) + (0.5 * scaled) * force))
        values.append(density * (scal[1, x, rows, :] + scaled * terms[1, x, rows, :]))
        values.append(density * scal[2, x, rows, :])
        values.append(density * (scal[3, x, rows, :] + scaled * terms[2, x, rows, :]))
        values.append(density * scal[4, x, rows, :])
        for f, value in enumerate(values):
            cons[cycle, f, x + 1, pl.ds(PAD + y0, TILE), :] = value
        pack_rows(cycle, 2, x, y0, values)
        return pack(h, x, edge, values), top

    present = jnp.zeros((1, nz), jnp.int32)
    block = lax.broadcasted_iota(jnp.int32, (1, nz), 1) // B
    for j in range(nz // B):
        value = mask_ref[index["gx"] * nx // B, index["gy"] * ny // B, index["gz"] * (nz // B) + j]
        present = jnp.where(block == j, value, present)

    def stage_remap(cycle, h, x, edge, top):
        y0 = 0
        rows = pl.ds(y0, TILE)
        active = jnp.broadcast_to(present, (TILE, nz)) > 0
        half_dt = 0.5 * step[0:1, :]
        velocity = [at(0, cycle, f, x, y0) for f in range(3)]
        z_ahead, z_behind = z_pair(cycle, 0, h, x, y0, 2, velocity[2])
        around = (
            (at(0, cycle, 0, x, y0, dx=1), at(0, cycle, 0, x, y0, dx=-1)),
            (at(0, cycle, 1, x, y0, dy=1), at(0, cycle, 1, x, y0, dy=-1)),
            (z_ahead, z_behind),
        )
        centre = 1.0
        into = []
        for j in range(3):
            upper = half_dt * (velocity[j] + around[j][0])
            lower = half_dt * (around[j][1] + velocity[j])
            up_in, down_in = jnp.minimum(upper, 0.0), jnp.maximum(lower, 0.0)
            centre = centre - (jnp.maximum(upper, 0.0) - jnp.minimum(lower, 0.0))
            into.append((up_in, down_in))

        def result(f):
            value = at(2, cycle, f, x, y0)
            ahead, behind = z_pair(cycle, 2, h, x, y0, f, value)
            return (
                centre * value
                - (into[0][0] * at(2, cycle, f, x, y0, dx=1) - into[0][1] * at(2, cycle, f, x, y0, dx=-1))
                - (into[1][0] * at(2, cycle, f, x, y0, dy=1) - into[1][1] * at(2, cycle, f, x, y0, dy=-1))
                - (into[2][0] * ahead - into[2][1] * behind)
            )

        density = result(0)
        inverse = 1.0 / density
        old = [scal[0, x, rows, :]] + velocity + [scal[n, x, rows, :] for n in range(1, 5)]
        new = [jnp.where(active, density, old[0])]
        for f in range(1, 8):
            new.append(jnp.where(active, result(f) * inverse, old[f]))
        if cycle == CYCLES - 1:
            for f in range(8):
                out_ref[f, x, rows, :] = new[f]
            return edge, top
        for n, f in enumerate((0, 4, 5, 6, 7)):
            scal[n, x, rows, :] = new[f]
        for f in range(3):
            vel[cycle + 1, f, x + 1, pl.ds(PAD + y0, TILE), :] = new[f + 1]
        inverse = jnp.where(active, inverse, inv[x, rows, :])
        inv[x, rows, :] = inverse
        return begin(cycle + 1, h, x, edge, top, new[0], inverse, new[4], new[1:4])

    def peak_copy(cycle, phase, away):
        axis = AXES[2 - phase]
        return pltpu.make_async_remote_copy(
            src_ref=peak.at[cycle, phase, 0],
            dst_ref=peak.at[cycle, phase, away],
            send_sem=peak_send.at[cycle, phase, away],
            recv_sem=peak_recv.at[cycle, phase, away],
            device_id={axis: lax.rem(index[axis] + away, sizes[axis])},
            device_id_type=MESH,
        )

    def peak_send_all(cycle, phase):
        for away in range(1, sizes[AXES[2 - phase]]):
            peak_copy(cycle, phase, away).start()

    def peak_take(cycle, phase):
        top = peak[cycle, phase, 0]
        for away in range(1, sizes[AXES[2 - phase]]):
            peak_copy(cycle, phase, away).wait_recv()
            top = jnp.maximum(top, peak[cycle, phase, away])
        if phase < 2:
            peak[cycle, phase + 1, 0] = top
        else:
            fastest = jnp.max(jnp.max(top, axis=1, keepdims=True), axis=0, keepdims=True)
            step[...] = courant / jnp.broadcast_to(fastest, step.shape)

    for load in loads:
        load.wait()
    pl.semaphore_wait(barrier, total)

    for h in range(HALVES):
        planes(h, stage_start, 0, (0, 0))
    for cycle in range(CYCLES):
        peak_send_all(cycle, 0)
        for h in range(HALVES):
            receive(cycle, 0, h)
            planes(h, functools.partial(stage_stress, cycle), cycle, (cycle, 1), 0)
            peak_take(cycle, h)
            peak_send_all(cycle, h + 1)
        peak_take(cycle, 2)
        for h in range(HALVES):
            receive(cycle, 1, h)
            planes(h, functools.partial(stage_conserved, cycle), cycle, (cycle, 2), 1)
        for h in range(HALVES):
            receive(cycle, 2, h)
            after = (cycle + 1, 0) if cycle + 1 < CYCLES else None
            planes(h, functools.partial(stage_remap, cycle), cycle, after, 2)

    for cycle in range(CYCLES):
        for phase in range(3):
            for away in range(1, sizes[AXES[2 - phase]]):
                peak_copy(cycle, phase, away).wait_send()
        for r in range(3):
            for s in range(2):
                way = above if s == 0 else below
                for_side(way["gx"], "gx", lambda: x_copy(cycle, r, s).wait_send())
                for h in range(HALVES):
                    for_side(way["gy"], "gy", lambda: y_copy(cycle, r, h, s).wait_send())
                    for_side(way["gz"], "gz", lambda: z_copy(cycle, r, h, s).wait_send())


def solution(mesh):
    sizes = {axis: mesh.shape[axis] for axis in AXES}

    def local(hydro_state, material_id, block_mask):
        _, nx, ny, nz = hydro_state.shape
        f32 = jnp.float32
        most = max(sizes.values())
        padded = (nx + 2, ny + 2 * PAD, nz)
        body = (nx, ny, nz)
        scratch = [
            pltpu.VMEM((CYCLES, 3) + padded, f32),
            pltpu.VMEM((CYCLES, 6) + padded, f32),
            pltpu.VMEM((CYCLES, 8) + padded, f32),
            pltpu.VMEM((5,) + body, f32),
            pltpu.VMEM(body, f32),
            pltpu.VMEM(body, jnp.int32),
            pltpu.VMEM(body, f32),
            pltpu.VMEM(body, f32),
            pltpu.VMEM((3,) + body, f32),
        ]
        for _ in range(2):
            scratch += [pltpu.VMEM((CYCLES, 2, count, nx, nz), f32) for count in COUNT]
        scratch += [
            pltpu.VMEM((CYCLES, 3, HALVES, ny, nz), f32),
            pltpu.VMEM((CYCLES, 3, HALVES, 2, ny, nz), f32),
            pltpu.VMEM((CYCLES, 3, HALVES, ny, nz), f32),
            pltpu.VMEM((CYCLES, 3, most, 8, nz), f32),
            pltpu.VMEM((8, nz), f32),
            pltpu.SemaphoreType.DMA((4,)),
            pltpu.SemaphoreType.DMA((CYCLES, 3, 2 + 4 * HALVES)),
            pltpu.SemaphoreType.DMA((CYCLES, 3, 2 + 4 * HALVES)),
            pltpu.SemaphoreType.DMA((CYCLES, 3, most)),
            pltpu.SemaphoreType.DMA((CYCLES, 3, most)),
        ]
        return pl.pallas_call(
            functools.partial(kernel, sizes),
            out_shape=jax.ShapeDtypeStruct(hydro_state.shape, f32),
            in_specs=[
                pl.BlockSpec(memory_space=pltpu.SMEM),
                pl.BlockSpec(memory_space=pl.ANY),
                pl.BlockSpec(memory_space=pl.ANY),
            ],
            out_specs=pl.BlockSpec(memory_space=pltpu.VMEM),
            scratch_shapes=scratch,
            compiler_params=pltpu.CompilerParams(
                collective_id=0, has_side_effects=True, vmem_limit_bytes=48 * 1024 * 1024
            ),
        )(block_mask, hydro_state, material_id)

    in_specs = (P(None, "gx", "gy", "gz"), P("gx", "gy", "gz"), P())
    out_specs = P(None, "gx", "gy", "gz")
    return jax.shard_map(local, mesh=mesh, in_specs=in_specs, out_specs=out_specs, check_vma=False)
```

```python
import functools

import jax
import jax.numpy as jnp
from jax import lax
from jax.experimental import pallas as pl
from jax.experimental.pallas import tpu as pltpu
from jax.sharding import PartitionSpec as P

B = 32
CYCLES = 2
AXES = ("gx", "gy", "gz")
HALVES = 2
PAD = 8
TILE = 32
GROUP = 2
MESH = pl.DeviceIdType.MESH

courant = 0.15
visc_quad = 2.0
visc_linear = 0.5
rest_density = (1.0, 1.25, 1.5, 1.8)
sound_base = (1.0, 0.8, 1.2, 0.9)
hugoniot_slope = (1.5, 1.4, 1.2, 1.6)
gruneisen = (2.0, 1.7, 1.6, 2.2)
stiffness = tuple(r * c * c for r, c in zip(rest_density, sound_base))

STRESS = ((0, 1, 2), (1, 3, 4), (2, 4, 5))
COUNT = (3, 3, 8)


def pick(is_one, is_two, is_three, table):
    return jnp.where(
        is_three, table[3], jnp.where(is_two, table[2], jnp.where(is_one, table[1], table[0]))
    )


def equation_of_state(density, inverse, energy, material):
    tests = (material == 1, material == 2, material == 3)
    rest_rho = pick(*tests, rest_density)
    sound_zero = pick(*tests, sound_base)
    slope = pick(*tests, hugoniot_slope)
    gamma = pick(*tests, gruneisen)
    stiff = pick(*tests, stiffness)
    strain = 1.0 - rest_rho * inverse
    climb = slope * jnp.maximum(strain, 0.0)
    hugoniot = stiff * strain * (1.0 + climb * (2.0 + 3.0 * climb))
    pressure = hugoniot * (1.0 - 0.5 * gamma * strain) + gamma * density * energy
    return pressure, sound_zero + sound_zero * climb


def kernel(
    sizes, mask_ref, state_hbm, material_hbm, out_ref,
    vel, stress, cons, scal, inv, mat, pres, sound, terms,
    ys0, ys1, ys2, yr0, yr1, yr2, zs, zr, zc, peak, step,
    load_sem, send_sem, recv_sem, peak_send, peak_recv,
):
    _, nx, ny, nz = state_hbm.shape
    half = nx // HALVES
    index = {axis: lax.axis_index(axis) for axis in AXES}
    above = {axis: index[axis] < sizes[axis] - 1 for axis in AXES}
    below = {axis: index[axis] > 0 for axis in AXES}
    ys, yr = (ys0, ys1, ys2), (yr0, yr1, yr2)
    buffers = (vel, stress, cons)
    inner = pl.ds(PAD, ny)

    loads = [
        pltpu.make_async_copy(state_hbm.at[1:4], vel.at[0, :, 1 : nx + 1, PAD : PAD + ny], load_sem.at[0]),
        pltpu.make_async_copy(state_hbm.at[0:1], scal.at[0:1], load_sem.at[1]),
        pltpu.make_async_copy(state_hbm.at[4:8], scal.at[1:5], load_sem.at[2]),
        pltpu.make_async_copy(material_hbm, mat, load_sem.at[3]),
    ]
    for load in loads:
        load.start()

    peers = (sizes["gz"], sizes["gx"] * sizes["gy"])

    def peer_at(phase, away):
        if phase == 0:
            return {"gz": lax.rem(index["gz"] + away, peers[0])}
        place = lax.rem(index["gx"] * sizes["gy"] + index["gy"] + away, peers[1])
        return {"gx": place // sizes["gy"], "gy": lax.rem(place, sizes["gy"])}

    barrier = pltpu.get_barrier_semaphore()
    total = 0
    for phase in range(2):
        for away in range(1, peers[phase]):
            pl.semaphore_signal(barrier, inc=1, device_id=peer_at(phase, away), device_id_type=MESH)
            total += 1

    for axis_number, axis in enumerate(AXES):
        for side, exists in ((0, below[axis]), (1, above[axis])):

            @pl.when(jnp.logical_not(exists))
            def _(axis_number=axis_number, side=side):
                for cycle in range(CYCLES):
                    for r in range(3):
                        if axis_number == 0:
                            ghost = (nx + 1) * side
                            for f in range(COUNT[r]):
                                buffers[r][cycle, f, ghost, inner, :] = jnp.zeros((ny, nz), jnp.float32)
                        elif axis_number == 1:
                            yr[r][cycle, side] = jnp.zeros(yr[r].shape[2:], jnp.float32)
                        else:
                            zr[cycle, r, :, side] = jnp.zeros((HALVES, ny, nz), jnp.float32)

    def copy(cycle, r, slot, side, src, dst, axis):
        move = 1 if side == 0 else sizes[axis] - 1
        return pltpu.make_async_remote_copy(
            src_ref=src,
            dst_ref=dst,
            send_sem=send_sem.at[cycle, r, slot],
            recv_sem=recv_sem.at[cycle, r, slot],
            device_id={axis: lax.rem(index[axis] + move, sizes[axis])},
            device_id_type=MESH,
        )

    def x_copy(cycle, r, side):
        own, ghost = (nx, 0) if side == 0 else (1, nx + 1)
        part = buffers[r].at[cycle, 0 : COUNT[r]]
        return copy(
            cycle, r, side, side,
            part.at[:, own, PAD : PAD + ny], part.at[:, ghost, PAD : PAD + ny], "gx",
        )

    def y_copy(cycle, r, h, side):
        rows = slice(h * half, (h + 1) * half)
        return copy(
            cycle, r, 2 + 4 * h + side, side,
            ys[r].at[cycle, side, :, rows], yr[r].at[cycle, side, :, rows], "gy",
        )

    def z_copy(cycle, r, h, side):
        return copy(
            cycle, r, 4 + 4 * h + side, side, zs.at[cycle, r, h], zr.at[cycle, r, h, side], "gz"
        )

    def for_side(exists, axis, act):
        if sizes[axis] > 1:
            pl.when(exists)(act)

    def send_x(cycle, r, side):
        for_side((above if side == 0 else below)["gx"], "gx", lambda: x_copy(cycle, r, side).start())

    def receive_x(cycle, r, side):
        for_side((below if side == 0 else above)["gx"], "gx", lambda: x_copy(cycle, r, side).wait_recv())

    def send(cycle, r, h):
        if h == 0:
            send_x(cycle, r, 1)
        for s in range(2):
            way = above if s == 0 else below
            for_side(way["gy"], "gy", lambda: y_copy(cycle, r, h, s).start())
            for_side(way["gz"], "gz", lambda: z_copy(cycle, r, h, s).start())

    lane = lax.broadcasted_iota(jnp.int32, (TILE, nz), 1)
    first_lane, last_lane = lane == 0, lane == nz - 1
    pair = lane // 2

    def receive(cycle, r, h):
        if h == 1:
            receive_x(cycle, r, 1)
        for s in range(2):
            way = below if s == 0 else above
            for_side(way["gy"], "gy", lambda: y_copy(cycle, r, h, s).wait_recv())
            for_side(way["gz"], "gz", lambda: z_copy(cycle, r, h, s).wait_recv())
        fields = STRESS[1] if r == 1 else range(COUNT[r])

        for x in range(h * half, h * half + half):
            for n, f in enumerate(fields):
                buffers[r][cycle, f, x + 1, pl.ds(PAD - 1, 1), :] = yr[r][cycle, 0, n, pl.ds(x, 1), :]
                buffers[r][cycle, f, x + 1, pl.ds(PAD + ny, 1), :] = yr[r][cycle, 1, n, pl.ds(x, 1), :]

        odd = lax.broadcasted_iota(jnp.int32, (ny, nz), 1) % 2 == 1
        zc[cycle, r, h] = jnp.where(
            odd, pltpu.roll(zr[cycle, r, h, 0], 1, 1), pltpu.roll(zr[cycle, r, h, 1], nz - 1, 1)
        )

    def pack(h, x, edge, values):
        for n, value in enumerate(values):
            slot = (x - h * half) * len(values) + n
            edge = jnp.where(pair == slot, pltpu.roll(value, 2 * slot + 1, 1), edge)
        return edge

    def pack_rows(cycle, r, x, y0, values):
        for n, value in enumerate(values):
            if y0 + TILE == ny:
                ys[r][cycle, 0, n, pl.ds(x, 1), :] = value[TILE - 1 : TILE]
            if y0 == 0:
                ys[r][cycle, 1, n, pl.ds(x, 1), :] = value[0:1]

    def at(r, cycle, f, x, y0, dx=0, dy=0):
        return buffers[r][cycle, f, x + 1 + dx, pl.ds(PAD + y0 + dy, TILE), :]

    def z_pair(cycle, r, h, x, y0, n, value):
        slot = (x - h * half) * COUNT[r] + n
        ghost = pltpu.roll(zc[cycle, r, h, pl.ds(y0, TILE), :], nz - 1 - 2 * slot, 1)
        ahead = jnp.where(last_lane, ghost, pltpu.roll(value, nz - 1, 1))
        behind = jnp.where(first_lane, ghost, pltpu.roll(value, 1, 1))
        return ahead, behind

    def planes(h, body, cycle, gives, takes=None):
        groups = half // GROUP

        def run(i, carry):
            edge, top = carry
            if h == 0 and takes is not None:
                pl.when(i == groups - 1)(lambda: receive_x(cycle, takes, 0))
            for j in range(GROUP):
                edge, top = body(h, (h + 1) * half - 1 - (i * GROUP + j), edge, top)
            if h == 1 and gives is not None:
                pl.when(i == 0)(lambda: send_x(gives[0], gives[1], 0))
            return edge, top

        init = (jnp.zeros((ny, nz), jnp.float32), jnp.zeros((8, nz), jnp.float32))
        edge, top = lax.fori_loop(0, groups, run, init)
        if gives is not None:
            zs[gives[0], gives[1], h] = edge
            if gives[1] == 0:
                peak[gives[0], 0, 0] = top if h == 0 else jnp.maximum(peak[gives[0], 0, 0], top)
            send(gives[0], gives[1], h)

    def begin(cycle, h, x, edge, top, density, inverse, energy, velocity):
        y0 = 0
        rows = pl.ds(y0, TILE)
        pressure, speed = equation_of_state(density, inverse, energy, mat[x, rows, :])
        pres[x, rows, :] = pressure
        sound[x, rows, :] = speed
        fast = speed + jnp.abs(velocity[0]) + jnp.abs(velocity[1]) + jnp.abs(velocity[2])
        for r0 in range(0, TILE, 8):
            top = jnp.maximum(top, fast[r0 : r0 + 8])
        pack_rows(cycle, 0, x, y0, velocity)
        return pack(h, x, edge, velocity), top

    def stage_start(h, x, edge, top):
        y0 = 0
        rows = pl.ds(y0, TILE)
        density = scal[0, x, rows, :]
        inverse = 1.0 / density
        inv[x, rows, :] = inverse
        return begin(0, h, x, edge, top, density, inverse, scal[1, x, rows, :], [at(0, 0, f, x, y0) for f in range(3)])

    def stage_stress(cycle, h, x, edge, top):
        y0 = 0
        rows = pl.ds(y0, TILE)
        g = []
        for f in range(3):
            ahead, behind = z_pair(cycle, 0, h, x, y0, f, at(0, cycle, f, x, y0))
            g.append((
                at(0, cycle, f, x, y0, dx=1) - at(0, cycle, f, x, y0, dx=-1),
                at(0, cycle, f, x, y0, dy=1) - at(0, cycle, f, x, y0, dy=-1),
                ahead - behind,
            ))
        div = 0.5 * (g[0][0] + g[1][1] + g[2][2])
        sxy, sxz, syz = g[0][1] + g[1][0], g[0][2] + g[2][0], g[1][2] + g[2][1]
        squares = 0.25 * (
            g[0][0] * g[0][0] + g[1][1] * g[1][1] + g[2][2] * g[2][2]
            + 0.5 * (sxy * sxy + sxz * sxz + syz * syz)
        )
        pressure = pres[x, rows, :]
        squash = jnp.maximum(-div, 0.0)
        mu = scal[0, x, rows, :] * squash * (visc_quad * squash + visc_linear * sound[x, rows, :])
        whole, quarter = 0.5 * mu, 0.25 * mu
        values = (
            whole * g[0][0] - pressure, quarter * sxy, quarter * sxz,
            whole * g[1][1] - pressure, quarter * syz, whole * g[2][2] - pressure,
        )
        for f, value in enumerate(values):
            stress[cycle, f, x + 1, pl.ds(PAD + y0, TILE), :] = value
        heat = mu * squares
        terms[0, x, rows, :] = div
        terms[1, x, rows, :] = heat - pressure * div
        terms[2, x, rows, :] = heat
        pack_rows(cycle, 1, x, y0, [values[f] for f in STRESS[1]])
        return pack(h, x, edge, [values[f] for f in STRESS[2]]), top

    def stage_conserved(cycle, h, x, edge, top):
        y0 = 0
        rows = pl.ds(y0, TILE)
        dt = step[0:1, :]
        inverse = inv[x, rows, :]
        scaled = dt * inverse
        density = scal[0, x, rows, :] / (1.0 + dt * terms[0, x, rows, :])
        values = [density]
        for i in range(3):
            fx, fy, fz = STRESS[i]
            ahead, behind = z_pair(cycle, 1, h, x, y0, i, at(1, cycle, fz, x, y0))
            force = (
                (at(1, cycle, fx, x, y0, dx=1) - at(1, cycle, fx, x, y0, dx=-1))
                + (at(1, cycle, fy, x, y0, dy=1) - at(1, cycle, fy, x, y0, dy=-1))
                + (ahead - behind)
            )
            values.append(density * (at(0, cycle, i, x, y0) + (0.5 * scaled) * force))
        values.append(density * (scal[1, x, rows, :] + scaled * terms[1, x, rows, :]))
        values.append(density * scal[2, x, rows, :])
        values.append(density * (scal[3, x, rows, :] + scaled * terms[2, x, rows, :]))
        values.append(density * scal[4, x, rows, :])
        for f, value in enumerate(values):
            cons[cycle, f, x + 1, pl.ds(PAD + y0, TILE), :] = value
        pack_rows(cycle, 2, x, y0, values)
        return pack(h, x, edge, values), top

    present = jnp.zeros((1, nz), jnp.int32)
    block = lax.broadcasted_iota(jnp.int32, (1, nz), 1) // B
    for j in range(nz // B):
        value = mask_ref[index["gx"] * nx // B, index["gy"] * ny // B, index["gz"] * (nz // B) + j]
        present = jnp.where(block == j, value, present)

    def stage_remap(cycle, h, x, edge, top):
        y0 = 0
        rows = pl.ds(y0, TILE)
        active = jnp.broadcast_to(present, (TILE, nz)) > 0
        half_dt = 0.5 * step[0:1, :]
        velocity = [at(0, cycle, f, x, y0) for f in range(3)]
        z_ahead, z_behind = z_pair(cycle, 0, h, x, y0, 2, velocity[2])
        around = (
            (at(0, cycle, 0, x, y0, dx=1), at(0, cycle, 0, x, y0, dx=-1)),
            (at(0, cycle, 1, x, y0, dy=1), at(0, cycle, 1, x, y0, dy=-1)),
            (z_ahead, z_behind),
        )
        centre = 1.0
        into = []
        for j in range(3):
            upper = half_dt * (velocity[j] + around[j][0])
            lower = half_dt * (around[j][1] + velocity[j])
            up_in, down_in = jnp.minimum(upper, 0.0), jnp.maximum(lower, 0.0)
            centre = centre - (jnp.maximum(upper, 0.0) - jnp.minimum(lower, 0.0))
            into.append((up_in, down_in))

        def result(f):
            value = at(2, cycle, f, x, y0)
            ahead, behind = z_pair(cycle, 2, h, x, y0, f, value)
            return (
                centre * value
                - (into[0][0] * at(2, cycle, f, x, y0, dx=1) - into[0][1] * at(2, cycle, f, x, y0, dx=-1))
                - (into[1][0] * at(2, cycle, f, x, y0, dy=1) - into[1][1] * at(2, cycle, f, x, y0, dy=-1))
                - (into[2][0] * ahead - into[2][1] * behind)
            )

        density = result(0)
        inverse = 1.0 / density
        old = [scal[0, x, rows, :]] + velocity + [scal[n, x, rows, :] for n in range(1, 5)]
        new = [jnp.where(active, density, old[0])]
        for f in range(1, 8):
            new.append(jnp.where(active, result(f) * inverse, old[f]))
        if cycle == CYCLES - 1:
            for f in range(8):
                out_ref[f, x, rows, :] = new[f]
            return edge, top
        for n, f in enumerate((0, 4, 5, 6, 7)):
            scal[n, x, rows, :] = new[f]
        for f in range(3):
            vel[cycle + 1, f, x + 1, pl.ds(PAD + y0, TILE), :] = new[f + 1]
        inverse = jnp.where(active, inverse, inv[x, rows, :])
        inv[x, rows, :] = inverse
        return begin(cycle + 1, h, x, edge, top, new[0], inverse, new[4], new[1:4])

    def peak_copy(cycle, phase, away):
        return pltpu.make_async_remote_copy(
            src_ref=peak.at[cycle, phase, 0],
            dst_ref=peak.at[cycle, phase, away],
            send_sem=peak_send.at[cycle, phase, away],
            recv_sem=peak_recv.at[cycle, phase, away],
            device_id=peer_at(phase, away),
            device_id_type=MESH,
        )

    def peak_send_all(cycle, phase):
        for away in range(1, peers[phase]):
            peak_copy(cycle, phase, away).start()

    def peak_take(cycle, phase):
        top = peak[cycle, phase, 0]
        for away in range(1, peers[phase]):
            peak_copy(cycle, phase, away).wait_recv()
            top = jnp.maximum(top, peak[cycle, phase, away])
        if phase < 1:
            peak[cycle, phase + 1, 0] = top
        else:
            fastest = jnp.max(jnp.max(top, axis=1, keepdims=True), axis=0, keepdims=True)
            step[...] = courant / jnp.broadcast_to(fastest, step.shape)

    for load in loads:
        load.wait()
    pl.semaphore_wait(barrier, total)

    for h in range(HALVES):
        planes(h, stage_start, 0, (0, 0))
    for cycle in range(CYCLES):
        peak_send_all(cycle, 0)
        for h in range(HALVES):
            receive(cycle, 0, h)
            planes(h, functools.partial(stage_stress, cycle), cycle, (cycle, 1), 0)
            if h == 0:
                peak_take(cycle, 0)
                peak_send_all(cycle, 1)
        for h in range(HALVES):
            receive(cycle, 1, h)
            if h == 0:
                peak_take(cycle, 1)
            planes(h, functools.partial(stage_conserved, cycle), cycle, (cycle, 2), 1)
        for h in range(HALVES):
            receive(cycle, 2, h)
            after = (cycle + 1, 0) if cycle + 1 < CYCLES else None
            planes(h, functools.partial(stage_remap, cycle), cycle, after, 2)

    for cycle in range(CYCLES):
        for phase in range(2):
            for away in range(1, peers[phase]):
                peak_copy(cycle, phase, away).wait_send()
        for r in range(3):
            for s in range(2):
                way = above if s == 0 else below
                for_side(way["gx"], "gx", lambda: x_copy(cycle, r, s).wait_send())
                for h in range(HALVES):
                    for_side(way["gy"], "gy", lambda: y_copy(cycle, r, h, s).wait_send())
                    for_side(way["gz"], "gz", lambda: z_copy(cycle, r, h, s).wait_send())


def solution(mesh):
    sizes = {axis: mesh.shape[axis] for axis in AXES}

    def local(hydro_state, material_id, block_mask):
        _, nx, ny, nz = hydro_state.shape
        f32 = jnp.float32
        most = max(sizes["gz"], sizes["gx"] * sizes["gy"])
        padded = (nx + 2, ny + 2 * PAD, nz)
        body = (nx, ny, nz)
        scratch = [
            pltpu.VMEM((CYCLES, 3) + padded, f32),
            pltpu.VMEM((CYCLES, 6) + padded, f32),
            pltpu.VMEM((CYCLES, 8) + padded, f32),
            pltpu.VMEM((5,) + body, f32),
            pltpu.VMEM(body, f32),
            pltpu.VMEM(body, jnp.int32),
            pltpu.VMEM(body, f32),
            pltpu.VMEM(body, f32),
            pltpu.VMEM((3,) + body, f32),
        ]
        for _ in range(2):
            scratch += [pltpu.VMEM((CYCLES, 2, count, nx, nz), f32) for count in COUNT]
        scratch += [
            pltpu.VMEM((CYCLES, 3, HALVES, ny, nz), f32),
            pltpu.VMEM((CYCLES, 3, HALVES, 2, ny, nz), f32),
            pltpu.VMEM((CYCLES, 3, HALVES, ny, nz), f32),
            pltpu.VMEM((CYCLES, 2, most, 8, nz), f32),
            pltpu.VMEM((8, nz), f32),
            pltpu.SemaphoreType.DMA((4,)),
            pltpu.SemaphoreType.DMA((CYCLES, 3, 2 + 4 * HALVES)),
            pltpu.SemaphoreType.DMA((CYCLES, 3, 2 + 4 * HALVES)),
            pltpu.SemaphoreType.DMA((CYCLES, 2, most)),
            pltpu.SemaphoreType.DMA((CYCLES, 2, most)),
        ]
        return pl.pallas_call(
            functools.partial(kernel, sizes),
            out_shape=jax.ShapeDtypeStruct(hydro_state.shape, f32),
            in_specs=[
                pl.BlockSpec(memory_space=pltpu.SMEM),
                pl.BlockSpec(memory_space=pl.ANY),
                pl.BlockSpec(memory_space=pl.ANY),
            ],
            out_specs=pl.BlockSpec(memory_space=pltpu.VMEM),
            scratch_shapes=scratch,
            compiler_params=pltpu.CompilerParams(
                collective_id=0, has_side_effects=True, vmem_limit_bytes=48 * 1024 * 1024
            ),
        )(block_mask, hydro_state, material_id)

    in_specs = (P(None, "gx", "gy", "gz"), P("gx", "gy", "gz"), P())
    out_specs = P(None, "gx", "gy", "gz")
    return jax.shard_map(local, mesh=mesh, in_specs=in_specs, out_specs=out_specs, check_vma=False)
```
